256 devices in a mesh: shot: 32 (over z, y_hi, core), rcv: 8 (over x, y_lo).
Axes of the slice: x: 4, y: 4 (y_hi: 2, y_lo: 2; y = y_hi * 2 + y_lo), z: 8, core: 2. Of those that a mesh axis runs over, the one named last changes fastest.
Arguments:
- left_traces: float32 [32, 4096, 2048], P('shot', 'rcv'), may hold values from -6 to 6
- right_traces: float32 [4096, 64, 2048], P('shot', 'rcv'), may hold values from -6 to 6
Outputs:
- multiples: float32 [32, 64, 2048], P('shot', 'rcv')
The draws below stay inside these ranges and needn't reach their ends.
All inputs are finite; a program needn't handle non-finite values.
Results may differ from the reference program's by a relative error of at most 0.0041.
Values may be sent and summed in bfloat16 or wider, within the bound.
No kernel may reach another device: no remote copies, remote signals or barrier semaphores. Data moves between devices by JAX's collectives and lax.ppermute only.
A program may use at most 320 MiB of HBM per device.

```python
import math
import jax
import jax.numpy as jnp
from jax import lax

K = 4096
NT = 2048
SW = 32
RW = 64
NF = 128
F_LO = 256


def level_of(own_key, extent, pieces, low, largest):
    def one(dim, parts):
        draws = jax.random.uniform(jax.random.fold_in(jax.random.fold_in(own_key, 6), dim), (parts,), jnp.float32, low / len(pieces), largest / len(pieces))
        return jnp.repeat(jnp.exp(draws), extent[dim] // parts).reshape((-1,) + (1,) * (len(extent) - dim - 1))

    factor_of = one(*pieces[0])
    for cut in pieces[1:]:
        factor_of = factor_of * one(*cut)
    return factor_of


def bell_draw(key, dims, scale, bound, shards=(), kind=jnp.bfloat16):
    gain = level_of(key, dims, shards, -0.22, 0.18) if shards else 1.0
    values = jax.random.normal(key, dims, jnp.float32) * scale * gain
    return jnp.minimum(jnp.maximum(values, -bound), bound).astype(kind)


def setup_inputs(seed: int = 0) -> dict:
    seeds = jax.random.split(jax.random.key(seed), 3)
    left_traces = bell_draw(seeds[0], (SW, K, NT), 1.0, 6.0, ((0, 32), (1, 8)), jnp.float32)
    right_traces = bell_draw(seeds[1], (K, RW, NT), 1.0, 6.0, ((0, 32), (1, 8)), jnp.float32)
    return dict(left_traces=left_traces, right_traces=right_traces)


def frequency_table(first_bin, bin_count, sample_count):
    bin_index = first_bin + jnp.arange(bin_count, dtype=jnp.int32)
    time_index = jnp.arange(sample_count, dtype=jnp.int32)
    phase_int = bin_index[:, None] * time_index[None, :] % sample_count
    radians = phase_int.astype(jnp.float32) * (2.0 * math.pi / sample_count)
    return jnp.concatenate([jnp.cos(radians), -jnp.sin(radians)], 0)

def reference(left_traces, right_traces):
    exact_arithmetic = lax.Precision.HIGHEST
    freq_table = frequency_table(F_LO, NF, NT)
    forward_table = freq_table * (1.0 / math.sqrt(NT))
    left_spec = jnp.einsum('ct,skt->csk', forward_table, left_traces, precision=exact_arithmetic).astype(jnp.bfloat16)
    right_spec = jnp.einsum('ct,krt->crk', forward_table, right_traces, precision=exact_arithmetic).astype(jnp.bfloat16)
    left_spec = lax.optimization_barrier(left_spec).astype(jnp.float32)
    right_spec = lax.optimization_barrier(right_spec).astype(jnp.float32)
    left_real_component, left_imaginary = (left_spec[:NF], left_spec[NF:])
    right_real_component, right_imaginary = (right_spec[:NF], right_spec[NF:])
    scale_multiplier = 1.0 / math.sqrt(K)
    real_component = (jnp.einsum('zhn,zqn->zhq', left_real_component, right_real_component, precision=exact_arithmetic) - jnp.einsum('zhn,zqn->zhq', left_imaginary, right_imaginary, precision=exact_arithmetic)) * scale_multiplier
    imaginary_component = (jnp.einsum('zhn,zqn->zhq', left_real_component, right_imaginary, precision=exact_arithmetic) + jnp.einsum('zhn,zqn->zhq', left_imaginary, right_real_component, precision=exact_arithmetic)) * scale_multiplier
    spectrum = jnp.concatenate([real_component, imaginary_component], 0)
    return jnp.einsum('csr,ct->srt', spectrum, freq_table, precision=exact_arithmetic) * math.sqrt(2.0 / NF)
```

```python
import math

import jax
import jax.numpy as jnp
import ml_dtypes
import numpy as np
from jax import lax
from jax.experimental import pallas as pl
from jax.experimental.pallas import tpu as pltpu
from jax.sharding import Mesh, PartitionSpec as P

K = 4096
NT = 2048
NF = 128
F_LO = 256
HALF = NT // 2
TB = 256
ALL = ("z", "yh", "core", "x", "yl")
PLANE = ("x", "yl", "yh", "core")


def bins_of_plane():
    even = F_LO + 2 * np.arange(NF // 2)
    return np.concatenate([even, even + 1]).reshape(32, 4)


def table_rows(bins):
    phase = (bins[..., None] * np.arange(NT)) % NT * (2.0 * np.pi / NT)
    return np.stack([np.cos(phase), -np.sin(phase)], -2)


def split_bf16(x):
    hi = x.astype(np.float32).astype(ml_dtypes.bfloat16)
    lo = (x - hi.astype(np.float64)).astype(np.float32).astype(ml_dtypes.bfloat16)
    return hi, lo


def dft_kernel(te_ref, to_ref, la_ref, lb_ref, ra0_ref, ra1_ref, rb0_ref, rb1_ref, out_ref, acc_ref):
    step = pl.program_id(0)
    nt = (((1,), (1,)), ((), ()))

    @pl.when(step == 0)
    def _():
        acc_ref[...] = jnp.zeros_like(acc_ref)

    for blk in range(6):
        if blk < 2:
            rows = pl.ds(blk * 256, 256)
            a, b = la_ref[rows, :], lb_ref[rows, :]
        else:
            r0 = 2 * (blk - 2)
            a, b = (
                jnp.concatenate(
                    [
                        jnp.concatenate([ref[pl.ds(r0 + n, 128, stride=8), :] for ref in refs], 1)
                        for n in range(2)
                    ],
                    0,
                )
                for refs in ((ra0_ref, ra1_ref), (rb0_ref, rb1_ref))
            )
        for half, t_ref in enumerate((te_ref, to_ref)):
            x = a - b if half else a + b
            hi = x.astype(jnp.bfloat16)
            lo = (x - hi.astype(jnp.float32)).astype(jnp.bfloat16)
            y = lax.dot_general(t_ref[...], hi, nt, preferred_element_type=jnp.float32)
            w = lax.dot_general(t_ref[:128, :], lo, nt, preferred_element_type=jnp.float32)
            acc_ref[half * 128 : half * 128 + 128, blk * 256 : blk * 256 + 256] += y[:128] + (y[128:] + w)

    @pl.when(step == pl.num_programs(0) - 1)
    def _():
        for blk in range(6):
            v = acc_ref[:, blk * 256 : blk * 256 + 256] * (1.0 / math.sqrt(NT))
            pair = [v[:, n * 128 : n * 128 + 128].reshape(32, 8, 128) for n in range(2)]
            out_ref[:, blk * 16 : blk * 16 + 16, :] = jnp.concatenate(pair, 1).astype(jnp.bfloat16)


def spectra(left, right, te, to):
    steps = HALF // TB
    lo_half, hi_half = (lambda i: (0, i)), (lambda i: (0, i + steps))
    return pl.pallas_call(
        dft_kernel,
        grid=(steps,),
        out_shape=jax.ShapeDtypeStruct((32, 96, 128), jnp.bfloat16),
        in_specs=[
            pl.BlockSpec((256, TB), lo_half),
            pl.BlockSpec((256, TB), lo_half),
            pl.BlockSpec((512, TB), lo_half),
            pl.BlockSpec((512, TB), hi_half),
            pl.BlockSpec((1024, 128), lambda i: (0, 2 * i)),
            pl.BlockSpec((1024, 128), lambda i: (0, 2 * i + 1)),
            pl.BlockSpec((1024, 128), lambda i: (0, 2 * (i + steps))),
            pl.BlockSpec((1024, 128), lambda i: (0, 2 * (i + steps) + 1)),
        ],
        out_specs=pl.BlockSpec((32, 96, 128), lambda i: (0, 0, 0)),
        scratch_shapes=[pltpu.VMEM((256, 1536), jnp.float32)],
        compiler_params=pltpu.CompilerParams(
            dimension_semantics=("arbitrary",), vmem_limit_bytes=40 * 2**20
        ),
        name="spectra",
    )(te, to, left, left, right, right, right, right)


def product_kernel(l_ref, g_ref, out_ref, lf_ref, rf_ref):
    lf_ref[...] = l_ref[...].astype(jnp.float32)
    for p in range(32):
        rf_ref[p * 64 : p * 64 + 64, :] = g_ref[p * 96 + 32 : p * 96 + 96, :].astype(jnp.float32)
    outs = []
    for f in range(4):
        left = [lf_ref[pl.ds(q * 8 + 2 * f + ri, 32, stride=32), :] for ri in range(2) for q in range(4)]
        lhs = jnp.concatenate(left, 1).astype(jnp.bfloat16)
        real_rows, imag_rows = [], []
        for yc in range(4):
            top, bottom = [], []
            for j in range(8):
                base = (j * 4 + yc) * 64 + 2 * f
                re = rf_ref[pl.ds(base, 8, stride=8), :]
                im = rf_ref[pl.ds(base + 1, 8, stride=8), :]
                top += [re, im]
                bottom += [-im, re]
            real_rows.append(jnp.concatenate(top, 0))
            imag_rows.append(jnp.concatenate(bottom, 0))
        rhs = jnp.concatenate(real_rows + imag_rows, 1).astype(jnp.bfloat16)
        outs.append(
            lax.dot_general(lhs, rhs, (((1,), (1,)), ((), ())), preferred_element_type=jnp.float32)
        )
    group = lax.broadcasted_iota(jnp.int32, (32, 128), 1) // 16
    for j in range(8):
        v = jnp.zeros((32, 128), jnp.float32)
        for f in range(4):
            moved = outs[f] if f == j else pltpu.roll(outs[f], (f - j) * 16 % 128, 1)
            v = jnp.where(group == f, moved, v)
        out_ref[pl.ds(j, 32, stride=8), :] = v


def product(left, gathered):
    return pl.pallas_call(
        product_kernel,
        out_shape=jax.ShapeDtypeStruct((256, 128), jnp.float32),
        scratch_shapes=[pltpu.VMEM((1024, 128), jnp.float32), pltpu.VMEM((2048, 128), jnp.float32)],
        compiler_params=pltpu.CompilerParams(vmem_limit_bytes=32 * 2**20),
        name="product",
    )(left, gathered)


def shards(left_traces, right_traces):
    table = table_rows(bins_of_plane())
    forward = table[..., :HALF].reshape(2, 128, HALF)
    te, to = (np.concatenate(split_bf16(forward[n]), 0) for n in range(2))
    sent = spectra(left_traces.reshape(512, NT), right_traces.reshape(1024, NT), te, to)
    here = lax.all_to_all(sent, PLANE, 0, 0, tiled=True)
    left = lax.all_to_all(here[:, :32, :].reshape(8, 128, 128), "z", 0, 0, tiled=True)
    part = product(left.reshape(1024, 128), here.reshape(3072, 128))
    parts = lax.all_to_all(part, ALL, 0, 0, tiled=True)
    spectrum = parts.reshape(8, 32, 128)[:, :, :64].sum(0).reshape(256, 8)
    inverse = table.reshape(8, 4, 8, NT).transpose(1, 0, 2, 3).reshape(256, NT).astype(np.float32)
    out = lax.dot_general(
        spectrum, inverse, (((0,), (0,)), ((), ())), precision=lax.Precision.HIGHEST
    ) * (math.sqrt(2.0 / NF) / math.sqrt(K))
    return out.reshape(1, 8, NT)


def solution(mesh):
    finer = Mesh(mesh.devices.reshape(8, 2, 2, 4, 2), ALL)
    placed = P(("z", "yh", "core"), ("x", "yl"), None)
    return jax.shard_map(
        shards, mesh=finer, in_specs=(placed, placed), out_specs=placed, check_vma=False
    )
```

```python
import math

import jax
import jax.numpy as jnp
import ml_dtypes
import numpy as np
from jax import lax
from jax.experimental import pallas as pl
from jax.experimental.pallas import tpu as pltpu
from jax.sharding import Mesh, PartitionSpec as P

K = 4096
NT = 2048
NF = 128
F_LO = 256
HALF = NT // 2
TB = 256
ALL = ("z", "yh", "core", "x", "yl")
PLANE = ("x", "yl", "yh", "core")


def bins_of_plane():
    even = F_LO + 2 * np.arange(NF // 2)
    return np.concatenate([even, even + 1]).reshape(32, 4)


def table_rows(bins):
    phase = (bins[..., None] * np.arange(NT)) % NT * (2.0 * np.pi / NT)
    return np.stack([np.cos(phase), -np.sin(phase)], -2)


def split_bf16(x):
    hi = x.astype(np.float32).astype(ml_dtypes.bfloat16)
    lo = (x - hi.astype(np.float64)).astype(np.float32).astype(ml_dtypes.bfloat16)
    return hi, lo


def spectra_kernel(w_hbm, l_hbm, r_hbm, out_ref, w_ref, l_ref, r_ref, acc_ref, sems):
    copies = []

    def copy(src, dst):
        copies.append(pltpu.make_async_copy(src, dst, sems.at[len(copies)]))
        return copies[-1]

    stages = []
    for c in range(4):
        spans = [pl.ds(n * HALF + c * TB, TB) for n in range(2)]
        stages.append([copy(r_hbm.at[:, span], r_ref.at[:, span]) for span in spans])
        stages[-1].append(copy(w_hbm.at[:, spans[0]], w_ref.at[:, spans[0]]))
    for c in range(2):
        rows = pl.ds(c * 256, 256)
        stages.append([copy(l_hbm.at[rows], l_ref.at[rows])])
    for stage in stages:
        for one in stage:
            one.start()

    def times_table(x, w):
        hi = x.astype(jnp.bfloat16)
        lo = (x - hi.astype(jnp.float32)).astype(jnp.bfloat16)
        y = jnp.dot(hi, w, preferred_element_type=jnp.float32)
        z = jnp.dot(lo, w[:, :128], preferred_element_type=jnp.float32)
        return y[:, :128] + (y[:, 128:] + z)

    def put(half, block, values):
        pair = [(v * (1.0 / math.sqrt(NT))).T.reshape(16, 8, 128) for v in values]
        rows = slice(block * 16, block * 16 + 16)
        out_ref[half * 16 : half * 16 + 16, rows, :] = jnp.concatenate(pair, 1).astype(jnp.bfloat16)

    for c in range(4):
        for one in stages[c]:
            one.wait()
        a = r_ref[:, c * TB : c * TB + TB]
        b = r_ref[:, HALF + c * TB : HALF + c * TB + TB]
        for half in range(2):
            y = times_table(a - b if half else a + b, w_ref[half, c * TB : c * TB + TB, :])
            if c == 0:
                acc_ref[half] = y
            else:
                acc_ref[half] += y
    for half in range(2):
        for n in range(4):
            put(half, 2 + n, [acc_ref[half, pl.ds(2 * n + m, 128, stride=8), :] for m in range(2)])
    for c in range(2):
        for one in stages[4 + c]:
            one.wait()
        a = l_ref[c * 256 : c * 256 + 256, :HALF]
        b = l_ref[c * 256 : c * 256 + 256, HALF:]
        for half in range(2):
            y = times_table(a - b if half else a + b, w_ref[half])
            put(half, c, [y[:128], y[128:]])


def spectra(left, right, table):
    return pl.pallas_call(
        spectra_kernel,
        out_shape=jax.ShapeDtypeStruct((32, 96, 128), jnp.bfloat16),
        in_specs=[pl.BlockSpec(memory_space=pl.ANY)] * 3,
        out_specs=pl.BlockSpec(memory_space=pltpu.VMEM),
        scratch_shapes=[
            pltpu.VMEM((2, HALF, 256), jnp.bfloat16),
            pltpu.VMEM((512, NT), jnp.float32),
            pltpu.VMEM((1024, NT), jnp.float32),
            pltpu.VMEM((2, 1024, 128), jnp.float32),
            pltpu.SemaphoreType.DMA((14,)),
        ],
        compiler_params=pltpu.CompilerParams(vmem_limit_bytes=60 * 2**20),
        name="spectra",
    )(table, left, right)


def product_kernel(l_ref, g_ref, out_ref, lf_ref, rf_ref):
    lf_ref[...] = l_ref[...].astype(jnp.float32)
    for p in range(32):
        rf_ref[p * 64 : p * 64 + 64, :] = g_ref[p * 96 + 32 : p * 96 + 96, :].astype(jnp.float32)
    outs = []
    for f in range(4):
        left = [lf_ref[pl.ds(q * 8 + 2 * f + ri, 32, stride=32), :] for ri in range(2) for q in range(4)]
        lhs = jnp.concatenate(left, 1).astype(jnp.bfloat16)
        real_rows, imag_rows = [], []
        for yc in range(4):
            top, bottom = [], []
            for j in range(8):
                base = (j * 4 + yc) * 64 + 2 * f
                re = rf_ref[pl.ds(base, 8, stride=8), :]
                im = rf_ref[pl.ds(base + 1, 8, stride=8), :]
                top += [re, im]
                bottom += [-im, re]
            real_rows.append(jnp.concatenate(top, 0))
            imag_rows.append(jnp.concatenate(bottom, 0))
        rhs = jnp.concatenate(real_rows + imag_rows, 1).astype(jnp.bfloat16)
        outs.append(
            lax.dot_general(lhs, rhs, (((1,), (1,)), ((), ())), preferred_element_type=jnp.float32)
        )
    group = lax.broadcasted_iota(jnp.int32, (32, 128), 1) // 16
    for j in range(8):
        v = jnp.zeros((32, 128), jnp.float32)
        for f in range(4):
            moved = outs[f] if f == j else pltpu.roll(outs[f], (f - j) * 16 % 128, 1)
            v = jnp.where(group == f, moved, v)
        out_ref[pl.ds(j, 32, stride=8), :] = v


def product(left, gathered):
    return pl.pallas_call(
        product_kernel,
        out_shape=jax.ShapeDtypeStruct((256, 128), jnp.float32),
        scratch_shapes=[pltpu.VMEM((1024, 128), jnp.float32), pltpu.VMEM((2048, 128), jnp.float32)],
        compiler_params=pltpu.CompilerParams(vmem_limit_bytes=32 * 2**20),
        name="product",
    )(left, gathered)


def inverse_kernel(parts_ref, hi_ref, lo_ref, out_ref):
    total = parts_ref[0:32, :]
    for z in range(1, 8):
        total = total + parts_ref[z * 32 : z * 32 + 32, :]
    turned = jnp.concatenate([total, jnp.zeros((96, 128), jnp.float32)], 0).T
    halves = []
    for n in range(2):
        part = turned[n * 32 : n * 32 + 8, :]
        for g in range(1, 4):
            row = n * 32 + g * 8
            part = part + pltpu.roll(turned[row : row + 8, :], g * 32, 1)
        halves.append(part)
    spectrum = jnp.concatenate(halves, 1)
    hi = spectrum.astype(jnp.bfloat16)
    lo = (spectrum - hi.astype(jnp.float32)).astype(jnp.bfloat16)
    y = jnp.dot(hi, hi_ref[...], preferred_element_type=jnp.float32)
    y = y + jnp.dot(lo, hi_ref[...], preferred_element_type=jnp.float32)
    y = y + jnp.dot(hi, lo_ref[...], preferred_element_type=jnp.float32)
    out_ref[...] = y * (math.sqrt(2.0 / NF) / math.sqrt(K))


def inverse(parts, hi, lo):
    return pl.pallas_call(
        inverse_kernel,
        out_shape=jax.ShapeDtypeStruct((8, NT), jnp.float32),
        compiler_params=pltpu.CompilerParams(vmem_limit_bytes=32 * 2**20),
        name="inverse",
    )(parts, hi, lo)


def shards(left_traces, right_traces):
    table = table_rows(bins_of_plane())
    forward = table[..., :HALF].reshape(2, 128, HALF)
    forward = np.stack([np.concatenate(split_bf16(one.T), 1) for one in forward])
    backward = table.reshape(8, 4, 8, NT).transpose(2, 1, 0, 3).reshape(256, NT)
    sent = spectra(left_traces.reshape(512, NT), right_traces.reshape(1024, NT), forward)
    here = lax.all_to_all(sent, PLANE, 0, 0, tiled=True)
    left = lax.all_to_all(here[:, :32, :].reshape(8, 128, 128), "z", 0, 0, tiled=True)
    part = product(left.reshape(1024, 128), here.reshape(3072, 128))
    parts = lax.all_to_all(part, ALL, 0, 0, tiled=True)
    return inverse(parts, *split_bf16(backward)).reshape(1, 8, NT)


def solution(mesh):
    finer = Mesh(mesh.devices.reshape(8, 2, 2, 4, 2), ALL)
    placed = P(("z", "yh", "core"), ("x", "yl"), None)
    return jax.shard_map(
        shards, mesh=finer, in_specs=(placed, placed), out_specs=placed, check_vma=False
    )
```

```python
import math

import jax
import jax.numpy as jnp
import ml_dtypes
import numpy as np
from jax import lax
from jax.experimental import pallas as pl
from jax.experimental.pallas import tpu as pltpu
from jax.sharding import Mesh, PartitionSpec as P

K = 4096
NT = 2048
NF = 128
F_LO = 256
HALF = NT // 2
TB = 256
AXES = ("za", "zb", "zc", "yh", "core", "xa", "xb", "yl")
Z = ("zb", "za", "zc")
PLANE = ("xb", "xa", "yl", "yh")


def bins_of_plane():
    even = F_LO + 2 * np.arange(NF // 2)
    return np.concatenate([even, even + 1]).reshape(16, 8)


def table_rows(bins):
    phase = (bins[..., None] * np.arange(NT)) % NT * (2.0 * np.pi / NT)
    return np.stack([np.cos(phase), -np.sin(phase)], -2)


def split_bf16(x):
    hi = x.astype(np.float32).astype(ml_dtypes.bfloat16)
    lo = (x - hi.astype(np.float64)).astype(np.float32).astype(ml_dtypes.bfloat16)
    return hi, lo


def spectra_kernel(w_hbm, l_hbm, r_hbm, out_ref, w_ref, l_ref, r_ref, acc_ref, sems):
    waits = []

    def fetch(src, dst, pieces):
        sem = sems.at[len(waits)]
        rows = src.shape[0] // pieces
        for n in range(pieces):
            part = pl.ds(n * rows, rows)
            pltpu.make_async_copy(src.at[part], dst.at[part], sem).start()
        waits.append(pltpu.make_async_copy(src, dst, sem))

    for c in range(4):
        spans = [pl.ds(n * HALF + c * TB, TB) for n in range(2)]
        fetch(w_hbm.at[:, spans[0]], w_ref.at[:, spans[0]], 1)
        for span in spans:
            fetch(r_hbm.at[:, span], r_ref.at[:, span], 8)
    fetch(l_hbm, l_ref, 16)

    def times_table(x, w):
        hi = x.astype(jnp.bfloat16)
        lo = (x - hi.astype(jnp.float32)).astype(jnp.bfloat16)
        y = jnp.dot(hi, w, preferred_element_type=jnp.float32)
        z = jnp.dot(lo, w[:, :128], preferred_element_type=jnp.float32)
        return y[:, :128] + (y[:, 128:] + z)

    def put(half, block, v):
        v = (v * (1.0 / math.sqrt(NT))).T.reshape(8, 16, 128)
        out_ref[half * 8 : half * 8 + 8, block * 16 : block * 16 + 16, :] = v.astype(jnp.bfloat16)

    for c in range(4):
        for one in waits[3 * c : 3 * c + 3]:
            one.wait()
        a = r_ref[:, c * TB : c * TB + TB]
        b = r_ref[:, HALF + c * TB : HALF + c * TB + TB]
        for half in range(2):
            y = times_table(a - b if half else a + b, w_ref[half, c * TB : c * TB + TB, :])
            if c == 0:
                acc_ref[half] = y
            else:
                acc_ref[half] += y
    for half in range(2):
        for r in range(8):
            put(half, 4 + r, acc_ref[half, pl.ds(r, 128, stride=8), :])
    waits[12].wait()
    a, b = l_ref[:, :HALF], l_ref[:, HALF:]
    for half in range(2):
        y = times_table(a - b if half else a + b, w_ref[half])
        for q in range(4):
            put(half, q, y[q * 128 : q * 128 + 128])


def spectra(left, right, table):
    return pl.pallas_call(
        spectra_kernel,
        out_shape=jax.ShapeDtypeStruct((16, 192, 128), jnp.bfloat16),
        in_specs=[pl.BlockSpec(memory_space=pl.ANY)] * 3,
        out_specs=pl.BlockSpec(memory_space=pltpu.VMEM),
        scratch_shapes=[
            pltpu.VMEM((2, HALF, 256), jnp.bfloat16),
            pltpu.VMEM((512, NT), jnp.float32),
            pltpu.VMEM((1024, NT), jnp.float32),
            pltpu.VMEM((2, 1024, 128), jnp.float32),
            pltpu.SemaphoreType.DMA((13,)),
        ],
        compiler_params=pltpu.CompilerParams(vmem_limit_bytes=60 * 2**20),
        name="spectra",
    )(table, left, right)


def product_kernel(l_ref, here_ref, there_ref, out_ref, lf_ref, rf_ref):
    own = lax.axis_index("core")
    lf_ref[...] = l_ref[...].astype(jnp.float32)
    for side, ref in enumerate((here_ref, there_ref)):
        for d in range(16):
            rows = slice(d * 128, d * 128 + 128)
            rf_ref[side, rows, :] = ref[d * 192 + 64 : d * 192 + 192, :].astype(jnp.float32)
    outs = []
    for f in range(8):
        left, real_rows, imag_rows = [[], []], [], []
        for side in range(2):
            core = own if side == 0 else 1 - own
            for yh in range(2):
                for ri in range(2):
                    row = yh * 32 + core * 16 + 2 * f + ri
                    shots = [lf_ref[pl.ds(row + n * 64, 8, stride=128), :] for n in range(2)]
                    left[ri].append(jnp.concatenate(shots, 0))
                top, bottom = [], []
                for j in range(8):
                    row = (j * 2 + yh) * 128 + 2 * f
                    re = rf_ref[side, pl.ds(row, 8, stride=16), :]
                    im = rf_ref[side, pl.ds(row + 1, 8, stride=16), :]
                    top += [re, im]
                    bottom += [-im, re]
                real_rows.append(jnp.concatenate(top, 0))
                imag_rows.append(jnp.concatenate(bottom, 0))
        lhs = jnp.concatenate(left[0] + left[1], 1).astype(jnp.bfloat16)
        rhs = jnp.concatenate(real_rows + imag_rows, 1).astype(jnp.bfloat16)
        outs.append(
            lax.dot_general(lhs, rhs, (((1,), (1,)), ((), ())), preferred_element_type=jnp.float32)
        )
    group = lax.broadcasted_iota(jnp.int32, (16, 128), 1) // 16
    for j in range(8):
        v = outs[j]
        for f in range(8):
            if f != j:
                v = jnp.where(group == f, pltpu.roll(outs[f], (f - j) * 16 % 128, 1), v)
        for yh in range(2):
            out_ref[pl.ds(j * 2 + yh, 8, stride=16), :] = v[yh * 8 : yh * 8 + 8]


def product(left, here, there):
    return pl.pallas_call(
        product_kernel,
        out_shape=jax.ShapeDtypeStruct((128, 128), jnp.float32),
        scratch_shapes=[pltpu.VMEM((1024, 128), jnp.float32), pltpu.VMEM((2, 2048, 128), jnp.float32)],
        compiler_params=pltpu.CompilerParams(vmem_limit_bytes=32 * 2**20),
        name="product",
    )(left, here, there)


def inverse_kernel(parts_ref, table_ref, out_ref):
    total = parts_ref[0:16, :]
    for z in range(1, 8):
        total = total + parts_ref[z * 16 : z * 16 + 16, :]
    turned = jnp.concatenate([total, jnp.zeros((112, 128), jnp.float32)], 0).T
    lane = lax.broadcasted_iota(jnp.int32, (8, 128), 1)
    sums = []
    for half in range(2):
        spectrum = jnp.zeros((8, 128), jnp.float32)
        for g in range(16):
            moved = pltpu.roll(turned[g * 8 : g * 8 + 8, :], (g - half) * 8 % 128, 1)
            spectrum = jnp.where(lane // 8 == g, moved, spectrum)
        hi = spectrum.astype(jnp.bfloat16)
        lo = (spectrum - hi.astype(jnp.float32)).astype(jnp.bfloat16)
        both = jnp.concatenate([hi.astype(jnp.float32), lo.astype(jnp.float32)], 0).astype(jnp.bfloat16)
        y = jnp.dot(both, table_ref[half, 0], preferred_element_type=jnp.float32)
        z = jnp.dot(both, table_ref[half, 1], preferred_element_type=jnp.float32)
        sums.append(y[:8] + (y[8:] + z[:8]))
    scale = math.sqrt(2.0 / NF) / math.sqrt(K)
    out_ref[:, :HALF] = (sums[0] + sums[1]) * scale
    out_ref[:, HALF:] = (sums[0] - sums[1]) * scale


def inverse(parts, table):
    return pl.pallas_call(
        inverse_kernel,
        out_shape=jax.ShapeDtypeStruct((8, NT), jnp.float32),
        compiler_params=pltpu.CompilerParams(vmem_limit_bytes=32 * 2**20),
        name="inverse",
    )(parts, table)


def shards(left_traces, right_traces):
    table = table_rows(bins_of_plane())[..., :HALF]
    forward = np.stack([np.concatenate(split_bf16(one.T), 1) for one in table.reshape(2, 128, HALF)])
    backward = table.reshape(2, 8, 16, HALF).transpose(0, 2, 1, 3).reshape(2, 128, HALF)
    backward = np.stack(split_bf16(backward), 1)
    sent = spectra(left_traces.reshape(512, NT), right_traces.reshape(1024, NT), forward)
    here = lax.all_to_all(sent, PLANE, 0, 0, tiled=True)
    there = lax.ppermute(here, "core", [(0, 1), (1, 0)])
    left = lax.all_to_all(here[:, :64, :].reshape(8, 128, 128), Z, 0, 0, tiled=True)
    part = product(left.reshape(1024, 128), here.reshape(3072, 128), there.reshape(3072, 128))
    parts = lax.all_to_all(part, Z + PLANE, 0, 0, tiled=True)
    return inverse(parts, backward).reshape(1, 8, NT)


def solution(mesh):
    finer = Mesh(mesh.devices.reshape((2,) * 8), AXES)
    placed = P(("za", "zb", "zc", "yh", "core"), ("xa", "xb", "yl"), None)
    return jax.shard_map(
        shards, mesh=finer, in_specs=(placed, placed), out_specs=placed, check_vma=False
    )
```

```python
import math

import jax
import jax.numpy as jnp
import ml_dtypes
import numpy as np
from jax import lax
from jax.experimental import pallas as pl
from jax.experimental.pallas import tpu as pltpu
from jax.sharding import Mesh, PartitionSpec as P

K = 4096
NT = 2048
NF = 128
F_LO = 256
HALF = NT // 2
TB = 256
AXES = ("za", "zb", "zc", "yh", "core", "xa", "xb", "yl")
Z = ("zb", "zc", "za")
PLANE = ("xb", "yl", "xa", "yh")


def bins_of_plane():
    even = F_LO + 2 * np.arange(NF // 2)
    return np.concatenate([even, even + 1]).reshape(16, 8)


def table_rows(bins):
    phase = (bins[..., None] * np.arange(NT)) % NT * (2.0 * np.pi / NT)
    return np.stack([np.cos(phase), -np.sin(phase)], -2)


def split_bf16(x):
    hi = x.astype(np.float32).astype(ml_dtypes.bfloat16)
    lo = (x - hi.astype(np.float64)).astype(np.float32).astype(ml_dtypes.bfloat16)
    return hi, lo


def spectra_kernel(w_hbm, l_hbm, r_hbm, out_ref, w_ref, l_ref, r_ref, acc_ref, sems):
    waits = []

    def fetch(src, dst, pieces):
        sem = sems.at[len(waits)]
        rows = src.shape[0] // pieces
        for n in range(pieces):
            part = pl.ds(n * rows, rows)
            pltpu.make_async_copy(src.at[part], dst.at[part], sem).start()
        waits.append(pltpu.make_async_copy(src, dst, sem))

    for c in range(4):
        spans = [pl.ds(n * HALF + c * TB, TB) for n in range(2)]
        fetch(w_hbm.at[:, spans[0]], w_ref.at[:, spans[0]], 1)
        for span in spans:
            fetch(r_hbm.at[:, span], r_ref.at[:, span], 8)
    fetch(l_hbm, l_ref, 16)

    def times_table(x, w):
        hi = x.astype(jnp.bfloat16)
        lo = (x - hi.astype(jnp.float32)).astype(jnp.bfloat16)
        y = jnp.dot(hi, w, preferred_element_type=jnp.float32)
        z = jnp.dot(lo, w[:, :128], preferred_element_type=jnp.float32)
        return y[:, :128] + (y[:, 128:] + z)

    def put(half, block, v):
        v = (v * (1.0 / math.sqrt(NT))).T.reshape(8, 16, 128)
        out_ref[half * 8 : half * 8 + 8, block * 16 : block * 16 + 16, :] = v.astype(jnp.bfloat16)

    for c in range(4):
        for one in waits[3 * c : 3 * c + 3]:
            one.wait()
        a = r_ref[:, c * TB : c * TB + TB]
        b = r_ref[:, HALF + c * TB : HALF + c * TB + TB]
        for half in range(2):
            y = times_table(a - b if half else a + b, w_ref[half, c * TB : c * TB + TB, :])
            if c == 0:
                acc_ref[half] = y
            else:
                acc_ref[half] += y
    for half in range(2):
        for r in range(8):
            rows = pl.ds(r, 128, stride=8)
            acc_ref[half, rows, :] = (acc_ref[half, rows, :] * (1.0 / math.sqrt(NT))).T
        turned = acc_ref[half].reshape(8, 128, 128).astype(jnp.bfloat16)
        out_ref[half * 8 : half * 8 + 8, 64:192, :] = turned
    waits[12].wait()
    a, b = l_ref[:, :HALF], l_ref[:, HALF:]
    for half in range(2):
        y = times_table(a - b if half else a + b, w_ref[half])
        for q in range(4):
            put(half, q, y[q * 128 : q * 128 + 128])


def spectra(left, right, table):
    return pl.pallas_call(
        spectra_kernel,
        out_shape=pltpu.VMEM((16, 192, 128), jnp.bfloat16),
        in_specs=[pl.BlockSpec(memory_space=pl.ANY)] * 3,
        out_specs=pl.BlockSpec(memory_space=pltpu.VMEM),
        scratch_shapes=[
            pltpu.VMEM((2, HALF, 256), jnp.bfloat16),
            pltpu.VMEM((512, NT), jnp.float32),
            pltpu.VMEM((1024, NT), jnp.float32),
            pltpu.VMEM((2, 1024, 128), jnp.float32),
            pltpu.SemaphoreType.DMA((13,)),
        ],
        compiler_params=pltpu.CompilerParams(vmem_limit_bytes=32 * 2**20),
        name="spectra",
    )(*(pltpu.with_memory_space_constraint(x, pltpu.HBM) for x in (table, left, right)))


def product_kernel(l_ref, here_ref, there_ref, out_ref, lf_ref):
    own = lax.axis_index("core")
    lf_ref[...] = l_ref[...].astype(jnp.float32)
    lane = lax.broadcasted_iota(jnp.int32, (16, 128), 1)
    outs = []
    for f in range(8):
        left, right = [[], []], []
        for side, ref in enumerate((here_ref, there_ref)):
            core = own if side == 0 else 1 - own
            for yh in range(2):
                for ri in range(2):
                    row = yh * 32 + core * 16 + 2 * f + ri
                    shots = [lf_ref[pl.ds(row + n * 64, 8, stride=128), :] for n in range(2)]
                    left[ri].append(jnp.concatenate(shots, 0))
                starts = [(j * 2 + yh) * 192 + 64 + f * 16 for j in range(8)]
                right.append(jnp.concatenate([ref[row : row + 16, :] for row in starts], 0))
        lhs = jnp.concatenate([jnp.concatenate(part, 1) for part in left], 0).astype(jnp.bfloat16)
        y = lax.dot_general(
            lhs,
            jnp.concatenate(right, 1),
            (((1,), (1,)), ((), ())),
            preferred_element_type=jnp.float32,
        )
        by_re, by_im = y[:16], y[16:]
        turned = jnp.where(lane % 16 < 8, -pltpu.roll(by_im, 120, 1), pltpu.roll(by_im, 8, 1))
        outs.append(by_re + turned)
    for j in range(8):
        v = outs[j]
        for f in range(8):
            if f != j:
                v = jnp.where(lane // 16 == f, pltpu.roll(outs[f], (f - j) * 16 % 128, 1), v)
        for yh in range(2):
            out_ref[pl.ds(j * 2 + yh, 8, stride=16), :] = v[yh * 8 : yh * 8 + 8]


def product(left, here, there):
    return pl.pallas_call(
        product_kernel,
        out_shape=jax.ShapeDtypeStruct((128, 128), jnp.float32),
        scratch_shapes=[pltpu.VMEM((1024, 128), jnp.float32)],
        compiler_params=pltpu.CompilerParams(vmem_limit_bytes=32 * 2**20),
        name="product",
    )(left, here, there)


def inverse_kernel(parts_ref, table_ref, out_ref):
    total = parts_ref[0:16, :]
    for z in range(1, 8):
        total = total + parts_ref[z * 16 : z * 16 + 16, :]
    turned = jnp.concatenate([total, jnp.zeros((112, 128), jnp.float32)], 0).T
    lane = lax.broadcasted_iota(jnp.int32, (8, 128), 1)
    sums = []
    for half in range(2):
        spectrum = jnp.zeros((8, 128), jnp.float32)
        for g in range(16):
            moved = pltpu.roll(turned[g * 8 : g * 8 + 8, :], (g - half) * 8 % 128, 1)
            spectrum = jnp.where(lane // 8 == g, moved, spectrum)
        hi = spectrum.astype(jnp.bfloat16)
        lo = (spectrum - hi.astype(jnp.float32)).astype(jnp.bfloat16)
        both = jnp.concatenate([hi.astype(jnp.float32), lo.astype(jnp.float32)], 0).astype(jnp.bfloat16)
        y = jnp.dot(both, table_ref[half, 0], preferred_element_type=jnp.float32)
        z = jnp.dot(both, table_ref[half, 1], preferred_element_type=jnp.float32)
        sums.append(y[:8] + (y[8:] + z[:8]))
    scale = math.sqrt(2.0 / NF) / math.sqrt(K)
    out_ref[:, :HALF] = (sums[0] + sums[1]) * scale
    out_ref[:, HALF:] = (sums[0] - sums[1]) * scale


def inverse(parts, table):
    return pl.pallas_call(
        inverse_kernel,
        out_shape=jax.ShapeDtypeStruct((8, NT), jnp.float32),
        compiler_params=pltpu.CompilerParams(vmem_limit_bytes=32 * 2**20),
        name="inverse",
    )(parts, table)


def shards(left_traces, right_traces):
    table = table_rows(bins_of_plane())[..., :HALF]
    forward = np.stack([np.concatenate(split_bf16(one.T), 1) for one in table.reshape(2, 128, HALF)])
    backward = table.reshape(2, 8, 16, HALF).transpose(0, 2, 1, 3).reshape(2, 128, HALF)
    backward = np.stack(split_bf16(backward), 1)
    sent = spectra(left_traces.reshape(512, NT), right_traces.reshape(1024, NT), forward)
    here = lax.all_to_all(sent, PLANE, 0, 0, tiled=True)
    there = lax.ppermute(here, "core", [(0, 1), (1, 0)])
    left = lax.all_to_all(here[:, :64, :].reshape(8, 128, 128), Z, 0, 0, tiled=True)
    part = product(left.reshape(1024, 128), here.reshape(3072, 128), there.reshape(3072, 128))
    parts = lax.all_to_all(part, Z + PLANE, 0, 0, tiled=True)
    return inverse(parts, backward).reshape(1, 8, NT)


def solution(mesh):
    finer = Mesh(mesh.devices.reshape((2,) * 8), AXES)
    placed = P(("za", "zb", "zc", "yh", "core"), ("xa", "xb", "yl"), None)
    return jax.shard_map(
        shards, mesh=finer, in_specs=(placed, placed), out_specs=placed, check_vma=False
    )
```

```python
import math

import jax
import jax.numpy as jnp
import ml_dtypes
import numpy as np
from jax import lax
from jax.experimental import pallas as pl
from jax.experimental.pallas import tpu as pltpu
from jax.sharding import Mesh, PartitionSpec as P

K = 4096
NT = 2048
NF = 128
F_LO = 256
HALF = NT // 2
TB = 256
AXES = ("za", "zb", "zc", "yh", "core", "xa", "xb", "yl")
Z = ("zb", "zc", "za")
PLANE = ("xb", "yl", "xa", "yh")


def bins_of_plane():
    even = F_LO + 2 * np.arange(NF // 2)
    return np.concatenate([even, even + 1]).reshape(16, 8)


def table_rows(bins):
    phase = (bins[..., None] * np.arange(NT)) % NT * (2.0 * np.pi / NT)
    return np.stack([np.cos(phase), -np.sin(phase)], -2)


def split_bf16(x):
    hi = x.astype(np.float32).astype(ml_dtypes.bfloat16)
    lo = (x - hi.astype(np.float64)).astype(np.float32).astype(ml_dtypes.bfloat16)
    return hi, lo


def spectra_kernel(w_hbm, l_hbm, r_hbm, out_ref, w_ref, l_ref, r_ref, acc_ref, sems):
    waits = []

    def fetch(src, dst, pieces):
        sem = sems.at[len(waits)]
        rows = src.shape[0] // pieces
        for n in range(pieces):
            part = pl.ds(n * rows, rows)
            pltpu.make_async_copy(src.at[part], dst.at[part], sem).start()
        waits.append(pltpu.make_async_copy(src, dst, sem))

    for c in range(4):
        spans = [pl.ds(n * HALF + c * TB, TB) for n in range(2)]
        fetch(w_hbm.at[:, spans[0]], w_ref.at[:, spans[0]], 1)
        for span in spans:
            fetch(r_hbm.at[:, span], r_ref.at[:, span], 8)
    fetch(l_hbm, l_ref, 16)

    def times_table(x, w):
        hi = x.astype(jnp.bfloat16)
        lo = (x - hi.astype(jnp.float32)).astype(jnp.bfloat16)
        y = jnp.dot(hi, w, preferred_element_type=jnp.float32)
        z = jnp.dot(lo, w[:, :128], preferred_element_type=jnp.float32)
        return y[:, :128] + (y[:, 128:] + z)

    def put(half, block, v):
        v = (v * (1.0 / math.sqrt(NT))).T.reshape(8, 16, 128)
        out_ref[half * 8 : half * 8 + 8, block * 16 : block * 16 + 16, :] = v.astype(jnp.bfloat16)

    for c in range(4):
        for one in waits[3 * c : 3 * c + 3]:
            one.wait()
        a = r_ref[:, c * TB : c * TB + TB]
        b = r_ref[:, HALF + c * TB : HALF + c * TB + TB]
        for half in range(2):
            y = times_table(a - b if half else a + b, w_ref[half, c * TB : c * TB + TB, :])
            if c == 0:
                acc_ref[half] = y
            else:
                acc_ref[half] += y
    for half in range(2):
        for r in range(8):
            rows = pl.ds(r, 128, stride=8)
            acc_ref[half, rows, :] = (acc_ref[half, rows, :] * (1.0 / math.sqrt(NT))).T
        turned = acc_ref[half].reshape(8, 128, 128).astype(jnp.bfloat16)
        out_ref[half * 8 : half * 8 + 8, 64:192, :] = turned
    waits[12].wait()
    a, b = l_ref[:, :HALF], l_ref[:, HALF:]
    for half in range(2):
        y = times_table(a - b if half else a + b, w_ref[half])
        for q in range(4):
            put(half, q, y[q * 128 : q * 128 + 128])


def spectra(left, right, table):
    return pl.pallas_call(
        spectra_kernel,
        out_shape=pltpu.VMEM((16, 192, 128), jnp.bfloat16),
        in_specs=[pl.BlockSpec(memory_space=pl.ANY)] * 3,
        out_specs=pl.BlockSpec(memory_space=pltpu.VMEM),
        scratch_shapes=[
            pltpu.VMEM((2, HALF, 256), jnp.bfloat16),
            pltpu.VMEM((512, NT), jnp.float32),
            pltpu.VMEM((1024, NT), jnp.float32),
            pltpu.VMEM((2, 1024, 128), jnp.float32),
            pltpu.SemaphoreType.DMA((13,)),
        ],
        compiler_params=pltpu.CompilerParams(vmem_limit_bytes=32 * 2**20),
        name="spectra",
    )(*(pltpu.with_memory_space_constraint(x, pltpu.HBM) for x in (table, left, right)))


def product_kernel(l_ref, here_ref, there_ref, out_ref, lf_ref):
    own = lax.axis_index("core")
    lf_ref[...] = l_ref[...].astype(jnp.float32)
    lane = lax.broadcasted_iota(jnp.int32, (16, 128), 1)
    outs = []
    for f in range(8):
        left, right = [[], []], []
        for side, (ref, height) in enumerate(((here_ref, 192), (there_ref, 128))):
            core = own if side == 0 else 1 - own
            for yh in range(2):
                for ri in range(2):
                    row = yh * 32 + core * 16 + 2 * f + ri
                    shots = [lf_ref[pl.ds(row + n * 64, 8, stride=128), :] for n in range(2)]
                    left[ri].append(jnp.concatenate(shots, 0))
                starts = [(j * 2 + yh + 1) * height - 128 + f * 16 for j in range(8)]
                right.append(jnp.concatenate([ref[row : row + 16, :] for row in starts], 0))
        lhs = jnp.concatenate([jnp.concatenate(part, 1) for part in left], 0).astype(jnp.bfloat16)
        y = lax.dot_general(
            lhs,
            jnp.concatenate(right, 1),
            (((1,), (1,)), ((), ())),
            preferred_element_type=jnp.float32,
        )
        by_re, by_im = y[:16], y[16:]
        turned = jnp.where(lane % 16 < 8, -pltpu.roll(by_im, 120, 1), pltpu.roll(by_im, 8, 1))
        outs.append(by_re + turned)
    for j in range(8):
        v = outs[j]
        for f in range(8):
            if f != j:
                v = jnp.where(lane // 16 == f, pltpu.roll(outs[f], (f - j) * 16 % 128, 1), v)
        for yh in range(2):
            out_ref[pl.ds(j * 2 + yh, 8, stride=16), :] = v[yh * 8 : yh * 8 + 8]


def product(left, here, there):
    return pl.pallas_call(
        product_kernel,
        out_shape=jax.ShapeDtypeStruct((128, 128), jnp.float32),
        scratch_shapes=[pltpu.VMEM((1024, 128), jnp.float32)],
        compiler_params=pltpu.CompilerParams(vmem_limit_bytes=32 * 2**20),
        name="product",
    )(left, here, there)


def inverse_kernel(parts_ref, table_ref, out_ref):
    total = parts_ref[0:16, :]
    for z in range(1, 8):
        total = total + parts_ref[z * 16 : z * 16 + 16, :]
    turned = jnp.concatenate([total, jnp.zeros((112, 128), jnp.float32)], 0).T
    lane = lax.broadcasted_iota(jnp.int32, (8, 128), 1)
    sums = []
    for half in range(2):
        spectrum = jnp.zeros((8, 128), jnp.float32)
        for g in range(16):
            moved = pltpu.roll(turned[g * 8 : g * 8 + 8, :], (g - half) * 8 % 128, 1)
            spectrum = jnp.where(lane // 8 == g, moved, spectrum)
        hi = spectrum.astype(jnp.bfloat16)
        lo = (spectrum - hi.astype(jnp.float32)).astype(jnp.bfloat16)
        both = jnp.concatenate([hi.astype(jnp.float32), lo.astype(jnp.float32)], 0).astype(jnp.bfloat16)
        y = jnp.dot(both, table_ref[half, 0], preferred_element_type=jnp.float32)
        z = jnp.dot(both, table_ref[half, 1], preferred_element_type=jnp.float32)
        sums.append(y[:8] + (y[8:] + z[:8]))
    scale = math.sqrt(2.0 / NF) / math.sqrt(K)
    out_ref[:, :HALF] = (sums[0] + sums[1]) * scale
    out_ref[:, HALF:] = (sums[0] - sums[1]) * scale


def inverse(parts, table):
    return pl.pallas_call(
        inverse_kernel,
        out_shape=jax.ShapeDtypeStruct((8, NT), jnp.float32),
        compiler_params=pltpu.CompilerParams(vmem_limit_bytes=32 * 2**20),
        name="inverse",
    )(parts, table)


def shards(left_traces, right_traces):
    table = table_rows(bins_of_plane())[..., :HALF]
    forward = np.stack([np.concatenate(split_bf16(one.T), 1) for one in table.reshape(2, 128, HALF)])
    backward = table.reshape(2, 8, 16, HALF).transpose(0, 2, 1, 3).reshape(2, 128, HALF)
    backward = np.stack(split_bf16(backward), 1)
    sent = spectra(left_traces.reshape(512, NT), right_traces.reshape(1024, NT), forward)
    here = lax.all_to_all(sent, PLANE, 0, 0, tiled=True)
    there = lax.ppermute(here[:, 64:, :], "core", [(0, 1), (1, 0)])
    left = lax.all_to_all(here[:, :64, :].reshape(8, 128, 128), Z, 0, 0, tiled=True)
    part = product(left.reshape(1024, 128), here.reshape(3072, 128), there.reshape(2048, 128))
    parts = lax.all_to_all(part, Z + PLANE, 0, 0, tiled=True)
    return inverse(parts, backward).reshape(1, 8, NT)


def solution(mesh):
    finer = Mesh(mesh.devices.reshape((2,) * 8), AXES)
    placed = P(("za", "zb", "zc", "yh", "core"), ("xa", "xb", "yl"), None)
    return jax.shard_map(
        shards, mesh=finer, in_specs=(placed, placed), out_specs=placed, check_vma=False
    )
```
